256 devices in a mesh: seq: 64 (over z, x, core), mp: 4 (over y).
Axes of the slice: x: 4, y: 4, z: 8, core: 2. Of those that a mesh axis runs over, the one named last changes fastest.
Arguments:
- tokens: bfloat16 [32768, 5120], P('seq'), may hold values from -6 to 6
- ln1_gain: float32 [5120], replicated, may hold values from 0.25 to 1.75
- w_query: bfloat16 [5120, 2560], P('seq', 'mp'), may hold values from -1 to 1
- w_key: bfloat16 [5120, 2560], P('seq', 'mp'), may hold values from -1 to 1
- w_value: bfloat16 [5120, 2560], P('seq', 'mp'), may hold values from -0.078125 to 0.078125
- w_out: bfloat16 [2560, 5120], P(None, 'mp'), may hold values from -0.125 to 0.125
- segment_ids: int32 [64, 512], P('seq'), may hold values from 0 to 7, never falling along the last dimension, each value on 1 to 256 neighbouring positions
- lnf_gain: float32 [5120], P('mp'), may hold values from 0.25 to 1.75
- w_pair: bfloat16 [5120, 64], P('mp'), may hold values from -0.078125 to 0.078125
- pair_start: int32 [1], replicated, may hold values from 0 to 32256
- residue_mask: int32 [512], replicated, may hold values 0 or 1
- w_pair_out: bfloat16 [64, 128], replicated, may hold values from -0.75 to 0.75
- rel_table: float32 [65, 128], replicated, may hold values from -6 to 6
- tri_gain: float32 [128], replicated, may hold values from 0.25 to 1.75
- w_ap: bfloat16 [128, 64], P(None, 'mp'), may hold values from -0.5 to 0.5
- w_ag: bfloat16 [128, 64], P(None, 'mp'), may hold values from -0.5 to 0.5
- w_bp: bfloat16 [128, 64], P(None, 'mp'), may hold values from -0.5 to 0.5
- w_bg: bfloat16 [128, 64], P(None, 'mp'), may hold values from -0.5 to 0.5
- w_gate: bfloat16 [128, 128], replicated, may hold values from -0.5 to 0.5
- out_gain: float32 [64], replicated, may hold values from 0.25 to 1.75
- w_tri_out: bfloat16 [64, 128], replicated, may hold values from -0.75 to 0.75
Outputs:
- final_states: bfloat16 [32768, 5120], P('seq', 'mp')
- pair_update: bfloat16 [512, 512, 128], P('seq', 'mp')
The draws below stay inside these ranges and needn't reach their ends.
Inputs may be any that keep to these rules, and one draw needn't show every extreme that they name: `segment_ids`: within each packed row the ids never fall; each protein has at most 256 tokens.
All inputs are finite; a program needn't handle non-finite values.
Results may differ from the reference program's by a relative error of at most 0.011.
Values may be sent and summed in bfloat16 or wider, within the bound.
No kernel may reach another device: no remote copies, remote signals or barrier semaphores. Data moves between devices by JAX's collectives and lax.ppermute only.
A program may use at most 128 MiB of HBM per device.

```python
import math
import jax
import jax.numpy as jnp
import numpy as np
from jax import lax

D = 5120
HEADS = 20
HD = 128
TOK_DEV = 512
TOKENS = 32768
RESIDUES = 512
QK = 32
CZ = 128
CH = 64
REL = 32
N_SEQ = 64


def column_field(key):
    return jax.random.normal(key, (D, HEADS * HD), jnp.float32)


def draw_tokens(key, part):
    key = jax.random.fold_in(key, 21)
    noise = jax.random.normal(key, (TOKENS, D), jnp.float32)
    values = noise
    return jnp.clip(values, -6.0, 6.0).astype(jnp.bfloat16)


def draw_w_query(key, part):
    common = column_field(key)
    private_key = jax.random.fold_in(key, 11)
    private = jax.random.normal(private_key, (D, HEADS * HD), jnp.float32)
    values = 0.95 * private + 0.3 * common
    return jnp.clip(values * D ** (-0.5), -1.0, 1.0).astype(jnp.bfloat16)


def draw_w_key(key, part):
    common = column_field(key)
    private_key = jax.random.fold_in(key, 12)
    private = jax.random.normal(private_key, (D, HEADS * HD), jnp.float32)
    values = 0.95 * private + 0.3 * common
    return jnp.clip(values * D ** (-0.5), -1.0, 1.0).astype(jnp.bfloat16)


def set_ends(array, rng, smallest, largest):
    shape = array.shape
    spot = [jax.random.randint(jax.random.fold_in(rng, axis), (), 0, shape[axis]) for axis in range(len(shape))]
    array = array.at[tuple(spot)].set(smallest)
    longest = shape.index(max(shape))
    spot[longest] = (spot[longest] + 1) % shape[longest]
    return array.at[tuple(spot)].set(largest)


def level_of(stream_key, extent, cuts, least, largest):
    factor_of = 1.0
    for dim, parts in cuts:
        heights = jax.random.uniform(jax.random.fold_in(jax.random.fold_in(stream_key, 6), dim), (parts,), jnp.float32, least / len(cuts), largest / len(cuts))
        factor_of = factor_of * jnp.repeat(jnp.exp(heights), extent[dim] // parts).reshape((-1,) + (1,) * (len(extent) - 1 - dim))
    return factor_of


def length_profile(amount, total, most, slope):
    weights = [(1 << 20) // math.isqrt(grade ** slope) + 1 for grade in range(2, amount + 1)]
    spare, given = total - most - (amount - 1), [1] * (amount - 1)
    while spare > 0:
        candidates = [i for i in range(amount - 1) if given[i] < most]
        whole, left = sum([weights[i] for i in candidates]), spare
        for i in candidates:
            addition = min(most - given[i], max(1, left * weights[i] // whole), spare)
            given[i] = given[i] + addition
            spare = spare - addition
    return np.array([most] + given)


def ragged_sizes(stream_key, number_of, total, most, lean):
    if number_of == 2:
        one = jax.random.randint(stream_key, (), max(1, total - most), min(most, total - 1) + 1)
        return jnp.stack([one, total - one])
    sizes = jnp.asarray(length_profile(number_of, total, most, lean), jnp.int32)
    couples = (number_of - 1) // 2
    giver, sink = sizes[1:1 + 2 * couples:2], sizes[2:2 + 2 * couples:2]
    room = jnp.minimum(giver - 1, most - sink)
    shifted = jax.random.randint(jax.random.fold_in(stream_key, 1), (couples,), 0, 1 << 20) % (room + 1)
    sizes = sizes.at[1:1 + 2 * couples:2].set(giver - shifted).at[2:2 + 2 * couples:2].set(sink + shifted)
    return sizes[jax.random.permutation(jax.random.fold_in(stream_key, 2), number_of)]


def centred(key, shape, scale, most, cuts=(), kind=jnp.bfloat16):
    loudness = level_of(key, shape, cuts, -0.22, 0.18) if cuts else 1.0
    values = jax.random.normal(key, shape, jnp.float32) * scale * loudness
    return jnp.minimum(jnp.maximum(values, -most), most).astype(kind)


def setup_inputs(seed: int = 0) -> dict:
    arg_keys = jax.random.split(jax.random.key(seed), 22)
    tokens = draw_tokens(jax.random.fold_in(arg_keys[21], 71), 0)
    ln1_gain = jnp.clip(1.0 + 0.15 * jax.random.normal(arg_keys[1], (D,), jnp.float32), 0.25, 1.75)
    w_query = draw_w_query(jax.random.fold_in(arg_keys[21], 71), 0)
    w_key = draw_w_key(jax.random.fold_in(arg_keys[21], 71), 0)
    w_value = centred(arg_keys[4], (D, HEADS * HD), D ** -0.5, 0.078125, ((0, 64), (1, 4)))
    w_out = centred(arg_keys[5], (HEADS * HD, D), (HEADS * HD) ** -0.5, 0.125, ((1, 4),))
    segment_ids = jax.vmap(lambda own: jnp.searchsorted(jnp.cumsum(ragged_sizes(own, max(3, min(8, TOK_DEV // 16)), TOK_DEV, TOK_DEV // 2, 1)), jnp.arange(TOK_DEV), side="right"))(jax.random.split(arg_keys[6], N_SEQ)).reshape((N_SEQ, TOK_DEV)).astype(jnp.int32)
    lnf_gain = jnp.clip(1.0 + 0.15 * jax.random.normal(arg_keys[7], (D,), jnp.float32), 0.25, 1.75)
    w_pair = centred(arg_keys[8], (D, 2 * QK), D ** -0.5, 0.078125, ((0, 4),))
    pair_start = jax.random.randint(arg_keys[9], (1,), 0, TOKENS - RESIDUES + 1).astype(jnp.int32)
    residue_mask = set_ends((jax.random.randint(arg_keys[10], (RESIDUES,), 0, 8) < 7).astype(jnp.int32), jax.random.fold_in(arg_keys[10], 1), 0, 1)
    w_pair_out = centred(arg_keys[11], (2 * QK, CZ), (2 * QK) ** -0.5, 0.75)
    rel_table = centred(arg_keys[12], (2 * REL + 1, CZ), 1.0, 6.0, (), jnp.float32)
    tri_gain = jnp.clip(1.0 + 0.15 * jax.random.normal(arg_keys[13], (CZ,), jnp.float32), 0.25, 1.75)
    w_ap = centred(arg_keys[14], (CZ, CH), CZ ** -0.5, 0.5, ((1, 4),))
    w_ag = centred(arg_keys[15], (CZ, CH), CZ ** -0.5, 0.5, ((1, 4),))
    w_bp = centred(arg_keys[16], (CZ, CH), CZ ** -0.5, 0.5, ((1, 4),))
    w_bg = centred(arg_keys[17], (CZ, CH), CZ ** -0.5, 0.5, ((1, 4),))
    w_gate = centred(arg_keys[18], (CZ, CZ), CZ ** -0.5, 0.5)
    out_gain = jnp.clip(1.0 + 0.15 * jax.random.normal(arg_keys[19], (CH,), jnp.float32), 0.25, 1.75)
    w_tri_out = centred(arg_keys[20], (CH, CZ), CH ** -0.5, 0.75)
    return dict(tokens=tokens, ln1_gain=ln1_gain, w_query=w_query, w_key=w_key, w_value=w_value, w_out=w_out, segment_ids=segment_ids, lnf_gain=lnf_gain, w_pair=w_pair, pair_start=pair_start, residue_mask=residue_mask, w_pair_out=w_pair_out, rel_table=rel_table, tri_gain=tri_gain, w_ap=w_ap, w_ag=w_ag, w_bp=w_bp, w_bg=w_bg, w_gate=w_gate, out_gain=out_gain, w_tri_out=w_tri_out)


EPS = 1e-05

def norm_rows(values, gain):
    center = values - lax.optimization_barrier(jnp.mean(values, axis=-1, keepdims=True))
    spread = lax.optimization_barrier(jnp.mean(center * center, axis=-1, keepdims=True))
    return center * lax.rsqrt(spread + EPS) * gain

def rotate(tensor, positions):
    half = tensor.shape[-1] // 2
    freqs = 10000.0 ** (-2.0 * jnp.arange(half, dtype=jnp.float32) / tensor.shape[-1])
    angles = positions.astype(jnp.float32)[:, None] * freqs[None, :]
    cosine = jnp.concatenate([jnp.cos(angles), jnp.cos(angles)], axis=-1)[:, None, :]
    sine = jnp.concatenate([jnp.sin(angles), jnp.sin(angles)], axis=-1)[:, None, :]
    turned = jnp.concatenate([-tensor[..., half:], tensor[..., :half]], axis=-1)
    return tensor * cosine + turned * sine

def attend(query_all, key_all, value_all, seg_row, head_dim):
    count = query_all.shape[0]
    heads = query_all.shape[1] // head_dim
    smaller = (seg_row[None, :] < seg_row[:, None]).astype(jnp.int32)
    positions = jnp.arange(count, dtype=jnp.int32) - lax.optimization_barrier(jnp.sum(smaller, axis=1))
    queries = rotate(query_all.reshape(count, heads, head_dim), positions).astype(jnp.bfloat16)
    key_rows = rotate(key_all.reshape(count, heads, head_dim), positions).astype(jnp.bfloat16)
    value_rows = value_all.reshape(count, heads, head_dim).astype(jnp.bfloat16)
    scores = jnp.einsum('qhd,khd->hqk', queries.astype(jnp.float32), key_rows.astype(jnp.float32)) * head_dim ** (-0.5)
    same = seg_row[:, None] == seg_row[None, :]
    scores = jnp.where(same[None, :, :], scores, -1e+30)
    top = lax.optimization_barrier(jnp.max(scores, axis=-1, keepdims=True))
    expo = jnp.exp(scores - top)
    weights = (expo / lax.optimization_barrier(jnp.sum(expo, axis=-1, keepdims=True))).astype(jnp.bfloat16)
    mixed = jnp.einsum('hqk,khd->qhd', weights.astype(jnp.float32), value_rows.astype(jnp.float32))
    return mixed.astype(jnp.bfloat16).reshape(count, heads * head_dim)

def pair_block(pair_in, start, count, w_pair_out, rel_table, tri_gain):
    width = pair_in.shape[1] // 2
    left = lax.dynamic_slice_in_dim(pair_in[:, :width], start, count, 0)
    right = pair_in[:, width:]
    total = right.shape[0]
    features = jnp.concatenate([left[:, None, :] * right[None, :, :], left[:, None, :] - right[None, :, :]], axis=-1)
    grid = jnp.einsum('ijf,fc->ijc', features, w_pair_out.astype(jnp.float32), precision=lax.Precision.HIGHEST)
    reach = (rel_table.shape[0] - 1) // 2
    offsets = jnp.arange(total, dtype=jnp.int32)[None, :] - (start + jnp.arange(count, dtype=jnp.int32))[:, None]
    bins = jnp.clip(offsets, -reach, reach) + reach
    onehot = (bins[..., None] == jnp.arange(rel_table.shape[0], dtype=jnp.int32)).astype(jnp.float32)
    grid = grid + jnp.einsum('ijr,rc->ijc', onehot, rel_table.astype(jnp.float32), precision=lax.Precision.HIGHEST)
    pair_grid = grid.astype(jnp.bfloat16)
    normed = norm_rows(pair_grid.astype(jnp.float32), tri_gain.astype(jnp.float32)).astype(jnp.bfloat16)
    return (pair_grid, normed)

def gated(normed, w_proj, w_gate_in, row_mask, col_mask):
    gate = jax.nn.sigmoid(jnp.dot(normed, w_gate_in, preferred_element_type=jnp.float32))
    projected = jnp.dot(normed, w_proj, preferred_element_type=jnp.float32)
    both = (row_mask[:, None] * col_mask[None, :])[..., None]
    return (gate * projected * both).astype(jnp.bfloat16)

def reference(tokens, ln1_gain, w_query, w_key, w_value, w_out, segment_ids, lnf_gain, w_pair, pair_start, residue_mask, w_pair_out, rel_table, tri_gain, w_ap, w_ag, w_bp, w_bg, w_gate, out_gain, w_tri_out):
    rows_in = tokens.reshape(N_SEQ, TOK_DEV, D)

    def one_row(packed):
        row_tokens, seg_row = packed
        normed = norm_rows(row_tokens.astype(jnp.float32), ln1_gain.astype(jnp.float32)).astype(jnp.bfloat16)
        query_all = jnp.dot(normed, w_query, preferred_element_type=jnp.float32)
        key_all = jnp.dot(normed, w_key, preferred_element_type=jnp.float32)
        value_all = jnp.dot(normed, w_value, preferred_element_type=jnp.float32)
        mixed = attend(query_all, key_all, value_all, seg_row, HD)
        result = row_tokens.astype(jnp.float32) + jnp.dot(mixed, w_out, preferred_element_type=jnp.float32)
        return result.astype(jnp.bfloat16)
    final_states = lax.map(one_row, (rows_in, segment_ids)).reshape(TOKENS, D)
    protein = lax.dynamic_slice_in_dim(final_states, pair_start[0], RESIDUES, 0)
    pair_in = jnp.dot(norm_rows(protein.astype(jnp.float32), lnf_gain.astype(jnp.float32)), w_pair.astype(jnp.float32), precision=lax.Precision.HIGHEST)
    pair_grid, normed = pair_block(pair_in, 0, RESIDUES, w_pair_out, rel_table, tri_gain)
    mask = residue_mask.astype(jnp.float32)
    left_side = gated(normed, w_ap, w_ag, mask, mask)
    right_side = gated(normed, w_bp, w_bg, mask, mask)
    gate_out = jax.nn.sigmoid(jnp.dot(normed, w_gate, preferred_element_type=jnp.float32))
    product = jnp.einsum('ikc,jkc->ijc', left_side.astype(jnp.float32), right_side.astype(jnp.float32), precision=lax.Precision.HIGHEST)
    update = jnp.einsum('ijc,cd->ijd', norm_rows(product, out_gain.astype(jnp.float32)), w_tri_out.astype(jnp.float32), precision=lax.Precision.HIGHEST)
    pair_update = (pair_grid.astype(jnp.float32) + gate_out * update).astype(jnp.bfloat16)
    return (final_states, pair_update)
```

```python
import functools

import jax
import jax.numpy as jnp
from jax import lax
from jax.experimental import pallas as pl
from jax.experimental.pallas import tpu as pltpu
from jax.sharding import Mesh, PartitionSpec as P

HD = 128
EPS = 1e-05
NZ, NX, NC, NY = 8, 4, 2, 4
SEQ = ("z", "x", "core")
F32, BF16 = jnp.float32, jnp.bfloat16


def shift(value, axis, size, by):
    return lax.ppermute(value, axis, [(i, (i + by) % size) for i in range(size)])


def partner(value, axis, size, bit):
    return lax.ppermute(value, axis, [(i, i ^ bit) for i in range(size)])


def split(value):
    high = lax.reduce_precision(value, 8, 7)
    return high.astype(BF16), (value - high).astype(BF16)


def norm_rows(values, gain):
    center = values - jnp.mean(values, axis=-1, keepdims=True)
    spread = jnp.mean(center * center, axis=-1, keepdims=True)
    return center * lax.rsqrt(spread + EPS) * gain


def rotate(tensor, positions):
    half = tensor.shape[-1] // 2
    freqs = 10000.0 ** (-2.0 * jnp.arange(half, dtype=F32) / tensor.shape[-1])
    angles = positions.astype(F32)[:, None] * freqs[None, :]
    cosine = jnp.concatenate([jnp.cos(angles), jnp.cos(angles)], axis=-1)[:, None, :]
    sine = jnp.concatenate([jnp.sin(angles), jnp.sin(angles)], axis=-1)[:, None, :]
    turned = jnp.concatenate([-tensor[..., half:], tensor[..., :half]], axis=-1)
    return tensor * cosine + turned * sine


def attend(query_all, key_all, value_all, seg_row, head_dim):
    count = query_all.shape[0]
    heads = query_all.shape[1] // head_dim
    smaller = (seg_row[None, :] < seg_row[:, None]).astype(jnp.int32)
    positions = jnp.arange(count, dtype=jnp.int32) - jnp.sum(smaller, axis=1)
    queries = rotate(query_all.reshape(count, heads, head_dim), positions).astype(BF16)
    key_rows = rotate(key_all.reshape(count, heads, head_dim), positions).astype(BF16)
    value_rows = value_all.reshape(count, heads, head_dim).astype(BF16)
    scores = jnp.einsum(
        "qhd,khd->hqk", queries, key_rows, preferred_element_type=F32
    ) * head_dim ** (-0.5)
    same = seg_row[:, None] == seg_row[None, :]
    scores = jnp.where(same[None, :, :], scores, -1e30)
    top = jnp.max(scores, axis=-1, keepdims=True)
    expo = jnp.exp(scores - top)
    weights = (expo / jnp.sum(expo, axis=-1, keepdims=True)).astype(BF16)
    mixed = jnp.einsum("hqk,khd->qhd", weights, value_rows, preferred_element_type=F32)
    return mixed.astype(BF16).reshape(count, heads * head_dim)


def pair_kernel(
    starts, left_ref, rrhs_ref, wp_ref, base_ref, wd_ref, rel_ref, gain_ref,
    wl_ref, wr_ref, wgate_ref, wout_ref, ogain_ref, mask_ref, mask_smem,
    out_ref, side_ref, own_x, own_n,
):
    n_i, n_j, _ = out_ref.shape
    res = rrhs_ref.shape[1]
    ch = side_ref.shape[1]
    i0, j0, tile, half = starts[0], starts[1], starts[2], starts[3]
    lane = lax.broadcasted_iota(jnp.int32, (128, 128), 1)
    const_lane = ((lane == 96) | (lane == 97)).astype(F32)
    low_lane = ((lane >= 64) & (lane < 96)) | (lane == 97)
    bins = lax.broadcasted_iota(jnp.int32, (64, res), 0)
    cols = lax.broadcasted_iota(jnp.int32, (64, res), 1)
    never = 4 * res
    diag = jnp.where(bins == 0, never, cols - bins)
    first_bin = jnp.where(bins == 0, cols, never)

    def grid_row(row):
        left = left_ref[pl.ds(row, 1), :]
        const = jnp.sum(left * wd_ref[...], axis=1, keepdims=True)
        full = left * wp_ref[...] + base_ref[...] + const * const_lane
        high = full.astype(BF16)
        low = (full - high.astype(F32)).astype(BF16)
        coef = jnp.where(low_lane, low.astype(F32), high.astype(F32)).astype(BF16)
        hot = (diag == row - 32) | (first_bin <= row - 32)
        hot = jnp.where(hot, 1.0, 0.0).astype(BF16)
        grid = jnp.dot(
            jnp.concatenate([coef, rel_ref[...]], axis=1),
            jnp.concatenate([rrhs_ref[...], hot, hot], axis=0),
            preferred_element_type=F32,
        )
        x = grid.astype(BF16)
        xf = x.astype(F32)
        center = xf - jnp.mean(xf, axis=0, keepdims=True)
        spread = jnp.mean(center * center, axis=0, keepdims=True)
        normed = (center * lax.rsqrt(spread + EPS) * gain_ref[...]).astype(BF16)
        return x, normed

    def side(normed, weight, row):
        both = jnp.dot(weight, normed, preferred_element_type=F32)
        gate = 0.5 + 0.5 * jnp.tanh(0.5 * both[:ch])
        keep = mask_ref[...] * mask_smem[row].astype(F32)
        return (gate * both[ch:] * keep).astype(BF16)

    def left_row(i, carry):
        x, normed = grid_row(i0 + i)
        side_ref[pl.ds(i, 1)] = side(normed, wl_ref[...], i0 + i)[None]
        own_x[pl.ds(i, 1)] = x[None]
        own_n[pl.ds(i, 1)] = normed[None]
        return carry

    def right_row(j, carry):
        normed = grid_row(j0 + j)[1]
        side_ref[pl.ds(n_i + j, 1)] = side(normed, wr_ref[...], j0 + j)[None]
        return carry

    lax.fori_loop(0, n_i, left_row, 0)
    lax.fori_loop(0, n_j, right_row, 0)

    left_side = jnp.swapaxes(side_ref[:n_i], 0, 1)
    right_side = jnp.swapaxes(side_ref[n_i:], 0, 1)
    product = lax.dot_general(
        left_side, right_side, (((2,), (2,)), ((0,), (0,))), preferred_element_type=F32
    )
    center = product - jnp.mean(product, axis=0, keepdims=True)
    spread = jnp.mean(center * center, axis=0, keepdims=True)
    hidden = center * lax.rsqrt(spread + EPS) * ogain_ref[...]
    hidden = jnp.swapaxes(hidden, 0, 1)
    window = pl.ds(pl.multiple_of(tile * 128, 128), 128)
    contract = (((0,), (0,)), ((), ()))

    def pick(value):
        return jnp.where(half == 0, value[:n_j], value[n_j:])

    for i in range(n_i):
        high = hidden[i].astype(BF16)
        low = (hidden[i] - high.astype(F32)).astype(BF16)
        update = lax.dot_general(
            jnp.concatenate([high, low], axis=0), wout_ref[...], contract,
            preferred_element_type=F32,
        )
        gate = lax.dot_general(
            own_n[i, :, window], wgate_ref[...], contract, preferred_element_type=F32
        )
        gate = 0.5 + 0.5 * jnp.tanh(0.5 * pick(gate))
        grid = pick(own_x[i, :, window].astype(F32).T)
        out_ref[i] = (grid + gate * update).astype(BF16)


def pair_phase(pair_t, w_pair_out, rel_table, tri_gain, sides, w_gate, w_tri_out, out_gain, mask):
    res = pair_t.shape[1]
    width = pair_t.shape[0] // 2
    core = lax.axis_index("core")
    plane = lax.axis_index("z") * NX + lax.axis_index("x")
    n_i, n_j = 16, 64
    starts = jnp.stack(
        [plane * n_i, lax.axis_index("mp") * 128 + core * n_j, lax.axis_index("mp"), core]
    ).astype(jnp.int32)
    left = pair_t[:width].T
    left3 = jnp.concatenate([left, left, left, jnp.zeros((res, 32), F32)], axis=1)
    right_high, right_low = split(pair_t[width:])
    rrhs = jnp.concatenate(
        [right_high, right_low, right_high, jnp.ones((2, res), BF16), jnp.zeros((30, res), BF16)],
        axis=0,
    )
    wp = w_pair_out[:width].astype(F32).T
    wd = w_pair_out[width:].astype(F32).T
    zero = jnp.zeros((128, 32), F32)
    wp3 = jnp.concatenate([wp, wp, wp, zero], axis=1)
    wd1 = jnp.concatenate([wd, zero, zero, zero], axis=1)
    last = rel_table[-1][:, None]
    base = jnp.concatenate([-wd, -wd, -wd, last, last, zero[:, :30]], axis=1)
    rel_high, rel_low = split((rel_table[:-1] - rel_table[-1:]).T)
    rel = jnp.concatenate([rel_high, rel_low], axis=1)
    smem = pl.BlockSpec(memory_space=pltpu.SMEM)
    vmem = pl.BlockSpec(memory_space=pltpu.VMEM)
    block = pl.pallas_call(
        pair_kernel,
        out_shape=jax.ShapeDtypeStruct((n_i, n_j, 128), BF16),
        in_specs=[smem] + [vmem] * 13 + [smem],
        out_specs=vmem,
        scratch_shapes=[
            pltpu.VMEM((n_i + n_j, 64, res), BF16),
            pltpu.VMEM((n_i, 128, res), BF16),
            pltpu.VMEM((n_i, 128, res), BF16),
        ],
        compiler_params=pltpu.CompilerParams(vmem_limit_bytes=48 * 2**20),
        name="pair_block",
    )(
        starts, left3, rrhs, wp3, base, wd1, rel, tri_gain[:, None],
        sides[0], sides[1], w_gate, jnp.concatenate([w_tri_out, w_tri_out], axis=0),
        out_gain[:, None, None], mask.astype(F32)[None], mask,
    )
    rows = n_i // 2
    theirs = lax.dynamic_slice_in_dim(block, (1 - core) * rows, rows, 0)
    own = lax.dynamic_slice_in_dim(block, core * rows, rows, 0)
    other = partner(theirs, "core", NC, 1)
    return jnp.where(
        core == 0, jnp.concatenate([own, other], axis=1), jnp.concatenate([other, own], axis=1)
    )


def pair_vectors(states, token_start, lnf_gain, w_pair, pair_start):
    count = states.shape[0]
    mp = lax.axis_index("mp")
    weight = lnf_gain[:, None] * w_pair.astype(F32)
    high, low = split(weight)
    table = jnp.concatenate([high, low, jnp.ones((weight.shape[0], 8), BF16)], axis=1)
    dots = lax.dot_general(table, states, (((0,), (1,)), ((), ())), preferred_element_type=F32)
    states32 = states.astype(F32)
    second = jnp.sum(states32 * states32, axis=1)
    lanes = count // NY
    shift_row = jnp.pad(jnp.sum(weight, axis=0), (0, lanes - 64))
    rows = jnp.concatenate([dots[:64] + dots[64:128], dots[128:129], second[None]], axis=0)
    parts = jnp.concatenate(
        [
            jnp.swapaxes(rows.reshape(66, NY, lanes), 0, 1),
            jnp.broadcast_to(shift_row, (NY, 1, lanes)),
            jnp.zeros((NY, 5, lanes), F32),
        ],
        axis=1,
    )
    total = lax.dynamic_index_in_dim(parts, mp, 0, False)
    for by in range(1, NY):
        total = total + shift(
            lax.dynamic_index_in_dim(parts, (mp + by) % NY, 0, False), "mp", NY, by
        )
    full_width = weight.shape[0] * NY
    center = total[64] / full_width
    spread = total[65] / full_width - center * center
    vectors = (total[:64] - total[66, :64][:, None] * center[None]) * lax.rsqrt(spread + EPS)[None]
    place = token_start + mp * lanes + jnp.arange(lanes, dtype=jnp.int32)
    wanted = (place >= pair_start) & (place < pair_start + count)
    vectors = jnp.where(wanted[None], vectors, 0.0)
    vectors = vectors + partner(vectors, "core", NC, 1)
    for bit in (1, 2):
        vectors = vectors + partner(vectors, "x", NX, bit)
    for bit in (1, 2, 4):
        vectors = vectors + partner(vectors, "z", NZ, bit)
    around = [vectors] + [shift(vectors, "mp", NY, -by) for by in range(1, NY)]
    ring = jnp.concatenate(around + around, axis=1)
    return lax.dynamic_slice_in_dim(ring, (pair_start - mp * lanes) % count, count, 1)


def shards(
    tokens,
    ln1_gain,
    w_query,
    w_key,
    w_value,
    w_out,
    segment_ids,
    lnf_gain,
    w_pair,
    pair_start,
    residue_mask,
    w_pair_out,
    rel_table,
    tri_gain,
    w_ap,
    w_ag,
    w_bp,
    w_bg,
    w_gate,
    out_gain,
    w_tri_out,
):
    mp_index = lax.axis_index("mp")
    seq_index = (lax.axis_index("z") * NX + lax.axis_index("x")) * NC + lax.axis_index("core")
    count = tokens.shape[0]
    normed_tokens = norm_rows(tokens.astype(F32), ln1_gain).astype(BF16)
    own = w_query.shape[1]
    weights = lax.all_gather(
        jnp.concatenate([w_query, w_key, w_value], axis=1), SEQ, axis=0, tiled=True
    )
    sides = lax.all_gather(jnp.stack([w_ag.T, w_ap.T, w_bg.T, w_bp.T]), "mp", axis=1, tiled=True)
    sides = (sides[:2].reshape(128, 128), sides[2:].reshape(128, 128))
    projected = jnp.dot(normed_tokens, weights, preferred_element_type=F32)
    mixed = attend(
        projected[:, :own], projected[:, own : 2 * own], projected[:, 2 * own :], segment_ids[0], HD
    )
    local_width = w_out.shape[1]
    total = lax.dynamic_slice_in_dim(tokens, mp_index * local_width, local_width, 1).astype(F32)
    for by in range(NY):
        block = shift(mixed, "mp", NY, by) if by else mixed
        rows = lax.dynamic_slice_in_dim(w_out, (mp_index - by) % NY * own, own, 0)
        total = total + jnp.dot(block, rows, preferred_element_type=F32)
    final_states = total.astype(BF16)
    pair_t = pair_vectors(final_states, seq_index * count, lnf_gain, w_pair, pair_start[0])
    pair_update = pair_phase(
        pair_t, w_pair_out, rel_table, tri_gain, sides, w_gate, w_tri_out, out_gain, residue_mask
    )
    return (final_states, pair_update)


def solution(mesh):
    split_mesh = Mesh(mesh.devices.reshape(NZ, NX, NC, NY), ("z", "x", "core", "mp"))
    return jax.shard_map(
        shards,
        mesh=split_mesh,
        in_specs=(
            P(SEQ, None),
            P(),
            P(SEQ, "mp"),
            P(SEQ, "mp"),
            P(SEQ, "mp"),
            P(None, "mp"),
            P(SEQ, None),
            P("mp"),
            P("mp", None),
            P(),
            P(),
            P(),
            P(),
            P(),
            P(None, "mp"),
            P(None, "mp"),
            P(None, "mp"),
            P(None, "mp"),
            P(),
            P(),
            P(),
        ),
        out_specs=(P(SEQ, "mp"), P(SEQ, "mp", None)),
        check_vma=False,
    )
```

```python
import functools

import jax
import jax.numpy as jnp
from jax import lax
from jax.experimental import pallas as pl
from jax.experimental.pallas import tpu as pltpu
from jax.sharding import Mesh, PartitionSpec as P

HD = 128
EPS = 1e-05
NZ, NX, NC, NY = 8, 4, 2, 4
SEQ = ("z", "x", "core")
F32, BF16 = jnp.float32, jnp.bfloat16


def shift(value, axis, size, by):
    return lax.ppermute(value, axis, [(i, (i + by) % size) for i in range(size)])


def partner(value, axis, size, bit):
    return lax.ppermute(value, axis, [(i, i ^ bit) for i in range(size)])


def split(value):
    high = lax.reduce_precision(value, 8, 7)
    return high.astype(BF16), (value - high).astype(BF16)


def norm_rows(values, gain):
    center = values - jnp.mean(values, axis=-1, keepdims=True)
    spread = jnp.mean(center * center, axis=-1, keepdims=True)
    return center * lax.rsqrt(spread + EPS) * gain


def angles_of(seg_rows, head_dim):
    smaller = (seg_rows[:, None, :] < seg_rows[:, :, None]).astype(jnp.int32)
    count = seg_rows.shape[1]
    positions = jnp.arange(count, dtype=jnp.int32)[None] - jnp.sum(smaller, axis=2)
    half = head_dim // 2
    freqs = 10000.0 ** (-2.0 * jnp.arange(half, dtype=F32) / head_dim)
    angles = positions.astype(F32)[:, :, None] * freqs
    cosine, sine = jnp.cos(angles), jnp.sin(angles)
    return (
        jnp.concatenate([cosine, cosine], axis=-1),
        jnp.concatenate([-sine, sine], axis=-1),
    )


def attend(query, key, value, cosine, sine, seg_rows):
    def turn(tensor):
        turned = jnp.concatenate([tensor[..., HD // 2 :], tensor[..., : HD // 2]], axis=-1)
        return (tensor * cosine + turned * sine).astype(BF16)

    queries, keys, values = turn(query), turn(key), value.astype(BF16)
    scores = jnp.einsum("rqd,rkd->rqk", queries, keys, preferred_element_type=F32) * HD ** (-0.5)
    scores = jnp.where(seg_rows[:, :, None] == seg_rows[:, None, :], scores, -1e30)
    expo = jnp.exp(scores - jnp.max(scores, axis=-1, keepdims=True))
    weights = (expo / jnp.sum(expo, axis=-1, keepdims=True)).astype(BF16)
    return jnp.einsum("rqk,rkd->rqd", weights, values, preferred_element_type=F32).astype(BF16)


def in_order(blocks, index, axis):
    count, size = len(blocks), blocks[0].shape[axis]
    double = jnp.concatenate(blocks + blocks, axis=axis)
    return lax.dynamic_slice_in_dim(double, (count - index) % count * size, count * size, axis)


def pair_kernel(
    starts, left_ref, rrhs_ref, wp_ref, base_ref, wd_ref, rel_ref, gain_ref,
    wl_ref, wr_ref, wgate_ref, wout_ref, ogain_ref, mask_ref, mask_smem,
    out_ref, side_ref, own_x, own_n,
):
    n_i, n_j, _ = out_ref.shape
    res = rrhs_ref.shape[1]
    ch = side_ref.shape[1]
    i0, j0, tile, half = starts[0], starts[1], starts[2], starts[3]
    lane = lax.broadcasted_iota(jnp.int32, (128, 128), 1)
    const_lane = ((lane == 96) | (lane == 97)).astype(F32)
    low_lane = ((lane >= 64) & (lane < 96)) | (lane == 97)
    bins = lax.broadcasted_iota(jnp.int32, (64, res), 0)
    cols = lax.broadcasted_iota(jnp.int32, (64, res), 1)
    never = 4 * res
    diag = jnp.where(bins == 0, never, cols - bins)
    first_bin = jnp.where(bins == 0, cols, never)

    def grid_row(row):
        left = left_ref[pl.ds(row, 1), :]
        const = jnp.sum(left * wd_ref[...], axis=1, keepdims=True)
        full = left * wp_ref[...] + base_ref[...] + const * const_lane
        high = full.astype(BF16)
        low = (full - high.astype(F32)).astype(BF16)
        coef = jnp.where(low_lane, low.astype(F32), high.astype(F32)).astype(BF16)
        hot = (diag == row - 32) | (first_bin <= row - 32)
        hot = jnp.where(hot, 1.0, 0.0).astype(BF16)
        grid = jnp.dot(
            jnp.concatenate([coef, rel_ref[...]], axis=1),
            jnp.concatenate([rrhs_ref[...], hot, hot], axis=0),
            preferred_element_type=F32,
        )
        x = grid.astype(BF16)
        xf = x.astype(F32)
        center = xf - jnp.mean(xf, axis=0, keepdims=True)
        spread = jnp.mean(center * center, axis=0, keepdims=True)
        normed = (center * lax.rsqrt(spread + EPS) * gain_ref[...]).astype(BF16)
        return x, normed

    def side(normed, weight, row):
        both = jnp.dot(weight, normed, preferred_element_type=F32)
        gate = 0.5 + 0.5 * jnp.tanh(0.5 * both[:ch])
        keep = mask_ref[...] * mask_smem[row].astype(F32)
        return (gate * both[ch:] * keep).astype(BF16)

    def left_row(i, carry):
        x, normed = grid_row(i0 + i)
        side_ref[pl.ds(i, 1)] = side(normed, wl_ref[...], i0 + i)[None]
        own_x[pl.ds(i, 1)] = x[None]
        own_n[pl.ds(i, 1)] = normed[None]
        return carry

    def right_row(j, carry):
        normed = grid_row(j0 + j)[1]
        side_ref[pl.ds(n_i + j, 1)] = side(normed, wr_ref[...], j0 + j)[None]
        return carry

    lax.fori_loop(0, n_i, left_row, 0, unroll=8)
    lax.fori_loop(0, n_j, right_row, 0, unroll=8)

    left_side = jnp.swapaxes(side_ref[:n_i], 0, 1)
    right_side = jnp.swapaxes(side_ref[n_i:], 0, 1)
    product = lax.dot_general(
        left_side, right_side, (((2,), (2,)), ((0,), (0,))), preferred_element_type=F32
    )
    center = product - jnp.mean(product, axis=0, keepdims=True)
    spread = jnp.mean(center * center, axis=0, keepdims=True)
    hidden = center * lax.rsqrt(spread + EPS) * ogain_ref[...]
    hidden = jnp.swapaxes(hidden, 0, 1)
    window = pl.ds(pl.multiple_of(tile * 128, 128), 128)
    contract = (((0,), (0,)), ((), ()))

    def pick(value):
        return jnp.where(half == 0, value[:n_j], value[n_j:])

    for i in range(n_i):
        high = hidden[i].astype(BF16)
        low = (hidden[i] - high.astype(F32)).astype(BF16)
        update = lax.dot_general(
            jnp.concatenate([high, low], axis=0), wout_ref[...], contract,
            preferred_element_type=F32,
        )
        gate = lax.dot_general(
            own_n[i, :, window], wgate_ref[...], contract, preferred_element_type=F32
        )
        gate = 0.5 + 0.5 * jnp.tanh(0.5 * pick(gate))
        grid = pick(own_x[i, :, window].astype(F32).T)
        out_ref[i] = (grid + gate * update).astype(BF16)


def pair_phase(pair_t, w_pair_out, rel_table, tri_gain, sides, w_gate, w_tri_out, out_gain, mask):
    res = pair_t.shape[1]
    width = pair_t.shape[0] // 2
    core = lax.axis_index("core")
    plane = lax.axis_index("z") * NX + lax.axis_index("x")
    n_i, n_j = 16, 64
    starts = jnp.stack(
        [plane * n_i, lax.axis_index("mp") * 128 + core * n_j, lax.axis_index("mp"), core]
    ).astype(jnp.int32)
    left = pair_t[:width].T
    left3 = jnp.concatenate([left, left, left, jnp.zeros((res, 32), F32)], axis=1)
    right_high, right_low = split(pair_t[width:])
    rrhs = jnp.concatenate(
        [right_high, right_low, right_high, jnp.ones((2, res), BF16), jnp.zeros((30, res), BF16)],
        axis=0,
    )
    wp = w_pair_out[:width].astype(F32).T
    wd = w_pair_out[width:].astype(F32).T
    zero = jnp.zeros((128, 32), F32)
    wp3 = jnp.concatenate([wp, wp, wp, zero], axis=1)
    wd1 = jnp.concatenate([wd, zero, zero, zero], axis=1)
    last = rel_table[-1][:, None]
    base = jnp.concatenate([-wd, -wd, -wd, last, last, zero[:, :30]], axis=1)
    rel_high, rel_low = split((rel_table[:-1] - rel_table[-1:]).T)
    rel = jnp.concatenate([rel_high, rel_low], axis=1)
    smem = pl.BlockSpec(memory_space=pltpu.SMEM)
    vmem = pl.BlockSpec(memory_space=pltpu.VMEM)
    block = pl.pallas_call(
        pair_kernel,
        out_shape=jax.ShapeDtypeStruct((n_i, n_j, 128), BF16),
        in_specs=[smem] + [vmem] * 13 + [smem],
        out_specs=vmem,
        scratch_shapes=[
            pltpu.VMEM((n_i + n_j, 64, res), BF16),
            pltpu.VMEM((n_i, 128, res), BF16),
            pltpu.VMEM((n_i, 128, res), BF16),
        ],
        compiler_params=pltpu.CompilerParams(vmem_limit_bytes=48 * 2**20),
        name="pair_block",
    )(
        starts, left3, rrhs, wp3, base, wd1, rel, tri_gain[:, None],
        sides[0], sides[1], w_gate, jnp.concatenate([w_tri_out, w_tri_out], axis=0),
        out_gain[:, None, None], mask.astype(F32)[None], mask,
    )
    rows = n_i // 2
    theirs = lax.dynamic_slice_in_dim(block, (1 - core) * rows, rows, 0)
    own = lax.dynamic_slice_in_dim(block, core * rows, rows, 0)
    other = partner(theirs, "core", NC, 1)
    return jnp.where(
        core == 0, jnp.concatenate([own, other], axis=1), jnp.concatenate([other, own], axis=1)
    )


def pair_vectors(states, token_start, lnf_gain, w_pair, pair_start):
    count = states.shape[0]
    mp = lax.axis_index("mp")
    weight = lnf_gain[:, None] * w_pair.astype(F32)
    high, low = split(weight)
    table = jnp.concatenate([high, low, jnp.ones((weight.shape[0], 8), BF16)], axis=1)
    dots = lax.dot_general(table, states, (((0,), (1,)), ((), ())), preferred_element_type=F32)
    states32 = states.astype(F32)
    second = jnp.sum(states32 * states32, axis=1)
    lanes = count // NY
    shift_row = jnp.pad(jnp.sum(weight, axis=0), (0, lanes - 64))
    rows = jnp.concatenate([dots[:64] + dots[64:128], dots[128:129], second[None]], axis=0)
    parts = jnp.concatenate(
        [
            jnp.swapaxes(rows.reshape(66, NY, lanes), 0, 1),
            jnp.broadcast_to(shift_row, (NY, 1, lanes)),
            jnp.zeros((NY, 5, lanes), F32),
        ],
        axis=1,
    )
    total = lax.dynamic_index_in_dim(parts, mp, 0, False)
    for by in range(1, NY):
        total = total + shift(
            lax.dynamic_index_in_dim(parts, (mp + by) % NY, 0, False), "mp", NY, by
        )
    full_width = weight.shape[0] * NY
    center = total[64] / full_width
    spread = total[65] / full_width - center * center
    vectors = (total[:64] - total[66, :64][:, None] * center[None]) * lax.rsqrt(spread + EPS)[None]
    place = token_start + mp * lanes + jnp.arange(lanes, dtype=jnp.int32)
    wanted = (place >= pair_start) & (place < pair_start + count)
    vectors = jnp.where(wanted[None], vectors, 0.0)
    vectors = vectors + partner(vectors, "core", NC, 1)
    vectors = sum([shift(vectors, "x", NX, by) for by in range(1, NX)], vectors)
    for bit in (1, 2, 4):
        vectors = vectors + partner(vectors, "z", NZ, bit)
    around = [vectors] + [shift(vectors, "mp", NY, -by) for by in range(1, NY)]
    ring = jnp.concatenate(around + around, axis=1)
    return lax.dynamic_slice_in_dim(ring, (pair_start - mp * lanes) % count, count, 1)


def shards(
    tokens,
    ln1_gain,
    w_query,
    w_key,
    w_value,
    w_out,
    segment_ids,
    lnf_gain,
    w_pair,
    pair_start,
    residue_mask,
    w_pair_out,
    rel_table,
    tri_gain,
    w_ap,
    w_ag,
    w_bp,
    w_bg,
    w_gate,
    out_gain,
    w_tri_out,
):
    mp_index = lax.axis_index("mp")
    seq_index = (lax.axis_index("z") * NX + lax.axis_index("x")) * NC + lax.axis_index("core")
    count = tokens.shape[0]

    groups = ((0, 3), (3, 5))
    columns = [
        held[:, first * HD : last * HD]
        for first, last in groups
        for held in (w_query, w_key, w_value)
    ]
    weights = lax.all_gather(jnp.concatenate(columns, axis=1), SEQ, axis=0, tiled=True)
    normed_tokens = norm_rows(tokens.astype(F32), ln1_gain).astype(BF16)
    sides = jnp.stack([w_ag.T, w_ap.T, w_bg.T, w_bp.T])
    sides = in_order([sides] + [shift(sides, "mp", NY, -by) for by in range(1, NY)], mp_index, 1)
    normed_tokens, sides = lax.optimization_barrier((normed_tokens, sides))
    sides = (sides[:2].reshape(128, 128), sides[2:].reshape(128, 128))
    cosine, sine = angles_of(segment_ids, HD)

    own = w_query.shape[1]
    local_width = w_out.shape[1]
    total = lax.dynamic_slice_in_dim(tokens, mp_index * local_width, local_width, 1).astype(F32)

    def exchange(mixed):
        half = count // 2
        up, down = shift(mixed, "mp", NY, 1), shift(mixed, "mp", NY, -1)
        far = jnp.concatenate(
            [shift(up[:half], "mp", NY, 1), shift(down[half:], "mp", NY, -1)], axis=0
        )
        return [(mixed, 0), (up, -1), (down, 1), (far, 2)]

    def output_part(total, mixed, start):
        for held, by in exchange(mixed):
            row = (mp_index + by) % NY * own + start
            rows = lax.dynamic_slice_in_dim(w_out, row, held.shape[1], 0)
            total = total + jnp.dot(held, rows, preferred_element_type=F32)
        return total

    def own_heads(rows, first, last):
        count = last - first
        cut = slice(first * 3 * HD, last * 3 * HD)
        projected = jnp.dot(rows, weights[:, cut], preferred_element_type=F32)
        heads = []
        for index in range(count):
            one = [
                projected[:, (part * count + index) * HD : (part * count + index + 1) * HD][None]
                for part in range(3)
            ]
            heads.append(attend(*one, cosine, sine, segment_ids)[0])
        return jnp.concatenate(heads, axis=1)

    mixed = own_heads(normed_tokens, *groups[0])
    total = output_part(total, mixed, 0)
    rows, mixed = lax.optimization_barrier((normed_tokens, mixed))
    total = output_part(total, own_heads(rows, *groups[1]), groups[1][0] * HD)
    final_states = total.astype(BF16)
    pair_t = pair_vectors(final_states, seq_index * count, lnf_gain, w_pair, pair_start[0])
    pair_update = pair_phase(
        pair_t, w_pair_out, rel_table, tri_gain, sides, w_gate, w_tri_out, out_gain, residue_mask
    )
    return (final_states, pair_update)


def solution(mesh):
    split_mesh = Mesh(mesh.devices.reshape(NZ, NX, NC, NY), ("z", "x", "core", "mp"))
    return jax.shard_map(
        shards,
        mesh=split_mesh,
        in_specs=(
            P(SEQ, None),
            P(),
            P(SEQ, "mp"),
            P(SEQ, "mp"),
            P(SEQ, "mp"),
            P(None, "mp"),
            P(SEQ, None),
            P("mp"),
            P("mp", None),
            P(),
            P(),
            P(),
            P(),
            P(),
            P(None, "mp"),
            P(None, "mp"),
            P(None, "mp"),
            P(None, "mp"),
            P(),
            P(),
            P(),
        ),
        out_specs=(P(SEQ, "mp"), P(SEQ, "mp", None)),
        check_vma=False,
    )
```

```python
import functools

import jax
import jax.numpy as jnp
from jax import lax
from jax.experimental import pallas as pl
from jax.experimental.pallas import tpu as pltpu
from jax.sharding import Mesh, PartitionSpec as P

HD = 128
EPS = 1e-05
NZ, NX, NC, NY = 8, 4, 2, 4
SEQ = ("z", "x", "core")
F32, BF16 = jnp.float32, jnp.bfloat16
BATCH, UNROLL = 4, 4


def shift(value, axis, size, by):
    return lax.ppermute(value, axis, [(i, (i + by) % size) for i in range(size)])


def partner(value, axis, size, bit):
    return lax.ppermute(value, axis, [(i, i ^ bit) for i in range(size)])


def split(value):
    high = lax.reduce_precision(value, 8, 7)
    return high.astype(BF16), (value - high).astype(BF16)


def norm_rows(values, gain):
    center = values - jnp.mean(values, axis=-1, keepdims=True)
    spread = jnp.mean(center * center, axis=-1, keepdims=True)
    return center * lax.rsqrt(spread + EPS) * gain


def angles_of(seg_rows, head_dim):
    smaller = (seg_rows[:, None, :] < seg_rows[:, :, None]).astype(jnp.int32)
    count = seg_rows.shape[1]
    positions = jnp.arange(count, dtype=jnp.int32)[None] - jnp.sum(smaller, axis=2)
    half = head_dim // 2
    freqs = 10000.0 ** (-2.0 * jnp.arange(half, dtype=F32) / head_dim)
    angles = positions.astype(F32)[:, :, None] * freqs
    cosine, sine = jnp.cos(angles), jnp.sin(angles)
    return (
        jnp.concatenate([cosine, cosine], axis=-1),
        jnp.concatenate([-sine, sine], axis=-1),
    )


def attend(query, key, value, cosine, sine, seg_rows):
    def turn(tensor):
        turned = jnp.concatenate([tensor[..., HD // 2 :], tensor[..., : HD // 2]], axis=-1)
        return (tensor * cosine + turned * sine).astype(BF16)

    queries, keys, values = turn(query), turn(key), value.astype(BF16)
    scores = jnp.einsum("rqd,rkd->rqk", queries, keys, preferred_element_type=F32) * HD ** (-0.5)
    scores = jnp.where(seg_rows[:, :, None] == seg_rows[:, None, :], scores, -1e30)
    expo = jnp.exp(scores - jnp.max(scores, axis=-1, keepdims=True))
    weights = (expo / jnp.sum(expo, axis=-1, keepdims=True)).astype(BF16)
    return jnp.einsum("rqk,rkd->rqd", weights, values, preferred_element_type=F32).astype(BF16)


def in_order(blocks, index, axis):
    count, size = len(blocks), blocks[0].shape[axis]
    double = jnp.concatenate(blocks + blocks, axis=axis)
    return lax.dynamic_slice_in_dim(double, (count - index) % count * size, count * size, axis)


def by_group(query, key, value, groups):
    def kernel(query_ref, key_ref, value_ref, out_ref):
        for first, last in groups:
            for place, held in enumerate((query_ref, key_ref, value_ref)):
                start = (first * 3 + place * (last - first)) * HD
                out_ref[:, start : start + (last - first) * HD] = held[:, first * HD : last * HD]

    vmem = pl.BlockSpec(memory_space=pltpu.VMEM)
    rows, width = query.shape
    return pl.pallas_call(
        kernel,
        out_shape=jax.ShapeDtypeStruct((rows, 3 * width), BF16),
        in_specs=[vmem] * 3,
        out_specs=vmem,
        name="by_group",
    )(query, key, value)


def pair_kernel(
    starts, left_ref, rrhs_ref, wp_ref, base_ref, wd_ref, rel_ref, gain_ref,
    wl_ref, wr_ref, wgate_ref, wout_ref, ogain_ref, mask_ref, mask_smem,
    out_ref, side_ref, own_x, own_n,
):
    n_i, n_j, _ = out_ref.shape
    res = rrhs_ref.shape[1]
    ch = side_ref.shape[1]
    i0, j0, tile, half = starts[0], starts[1], starts[2], starts[3]
    lane = lax.broadcasted_iota(jnp.int32, (128, 128), 1)
    const_lane = ((lane == 96) | (lane == 97)).astype(F32)
    low_lane = ((lane >= 64) & (lane < 96)) | (lane == 97)
    span = res + 128

    def coefficients(row):
        left = left_ref[pl.ds(row, 1), :]
        const = jnp.sum(left * wd_ref[...], axis=1, keepdims=True)
        full = left * wp_ref[...] + base_ref[...] + const * const_lane
        high = full.astype(BF16).astype(F32)
        return jnp.where(low_lane, full - high, high).astype(BF16)

    def relative(row):
        start = res - row
        rest = lax.rem(start, 128)
        slab = rel_ref[:, pl.ds(pl.multiple_of(start - rest, 128), span)]
        return pltpu.roll(slab, lax.rem(span - rest, span), 1)[:, :res]

    def grid_rows(first):
        dots = jnp.dot(
            jnp.concatenate([coefficients(first + r) for r in range(BATCH)], axis=0),
            rrhs_ref[...],
            preferred_element_type=F32,
        )
        rows = []
        for r in range(BATCH):
            x = (dots[r * 128 : (r + 1) * 128] + relative(first + r)).astype(BF16)
            xf = x.astype(F32)
            center = xf - jnp.mean(xf, axis=0, keepdims=True)
            spread = jnp.mean(center * center, axis=0, keepdims=True)
            rows.append((x, (center * lax.rsqrt(spread + EPS) * gain_ref[...]).astype(BF16)))
        return rows

    def side(normed, weight, row):
        both = jnp.dot(weight, normed, preferred_element_type=F32)
        gate = 0.5 + 0.5 * jnp.tanh(0.5 * both[:ch])
        keep = mask_ref[...] * mask_smem[row].astype(F32)
        return (gate * both[ch:] * keep).astype(BF16)

    def left_rows(step, carry):
        for r, (x, normed) in enumerate(grid_rows(i0 + step * BATCH)):
            i = step * BATCH + r
            side_ref[pl.ds(i, 1)] = side(normed, wl_ref[...], i0 + i)[None]
            own_x[pl.ds(i, 1)] = x[None]
            own_n[pl.ds(i, 1)] = normed[None]
        return carry

    def right_rows(step, carry):
        for r, (_, normed) in enumerate(grid_rows(j0 + step * BATCH)):
            j = step * BATCH + r
            side_ref[pl.ds(n_i + j, 1)] = side(normed, wr_ref[...], j0 + j)[None]
        return carry

    lax.fori_loop(0, n_i // BATCH, left_rows, 0, unroll=UNROLL)
    lax.fori_loop(0, n_j // BATCH, right_rows, 0, unroll=UNROLL)

    left_side = jnp.swapaxes(side_ref[:n_i], 0, 1)
    right_side = jnp.swapaxes(side_ref[n_i:], 0, 1)
    product = lax.dot_general(
        left_side, right_side, (((2,), (2,)), ((0,), (0,))), preferred_element_type=F32
    )
    center = product - jnp.mean(product, axis=0, keepdims=True)
    spread = jnp.mean(center * center, axis=0, keepdims=True)
    hidden = center * lax.rsqrt(spread + EPS) * ogain_ref[...]
    hidden = jnp.swapaxes(hidden, 0, 1)
    window = pl.ds(pl.multiple_of(tile * 128, 128), 128)
    contract = (((0,), (0,)), ((), ()))

    def pick(value):
        return jnp.where(half == 0, value[:n_j], value[n_j:])

    for i in range(n_i):
        high = hidden[i].astype(BF16)
        low = (hidden[i] - high.astype(F32)).astype(BF16)
        update = lax.dot_general(
            jnp.concatenate([high, low], axis=0), wout_ref[...], contract,
            preferred_element_type=F32,
        )
        gate = lax.dot_general(
            own_n[i, :, window], wgate_ref[...], contract, preferred_element_type=F32
        )
        gate = 0.5 + 0.5 * jnp.tanh(0.5 * pick(gate))
        grid = pick(own_x[i, :, window].astype(F32).T)
        out_ref[i] = (grid + gate * update).astype(BF16)


def pair_phase(pair_t, w_pair_out, rel_table, tri_gain, sides, w_gate, w_tri_out, out_gain, mask):
    res = pair_t.shape[1]
    width = pair_t.shape[0] // 2
    core = lax.axis_index("core")
    plane = lax.axis_index("z") * NX + lax.axis_index("x")
    n_i, n_j = 16, 64
    starts = jnp.stack(
        [plane * n_i, lax.axis_index("mp") * 128 + core * n_j, lax.axis_index("mp"), core]
    ).astype(jnp.int32)
    left = pair_t[:width].T
    left3 = jnp.concatenate([left, left, left, jnp.zeros((res, 32), F32)], axis=1)
    right_high, right_low = split(pair_t[width:])
    rrhs = jnp.concatenate(
        [right_high, right_low, right_high, jnp.ones((2, res), BF16), jnp.zeros((30, res), BF16)],
        axis=0,
    )
    wp = w_pair_out[:width].astype(F32).T
    wd = w_pair_out[width:].astype(F32).T
    zero = jnp.zeros((128, 32), F32)
    wp3 = jnp.concatenate([wp, wp, wp, zero], axis=1)
    wd1 = jnp.concatenate([wd, zero, zero, zero], axis=1)
    base = jnp.concatenate([-wd, -wd, -wd, zero], axis=1)
    table = rel_table.T
    reach = (rel_table.shape[0] - 1) // 2
    rel = jnp.concatenate(
        [
            jnp.broadcast_to(table[:, :1], (128, res - reach + 1)),
            table[:, 1:],
            jnp.broadcast_to(table[:, -1:], (128, res + 127 - reach)),
        ],
        axis=1,
    )
    smem = pl.BlockSpec(memory_space=pltpu.SMEM)
    vmem = pl.BlockSpec(memory_space=pltpu.VMEM)
    block = pl.pallas_call(
        pair_kernel,
        out_shape=jax.ShapeDtypeStruct((n_i, n_j, 128), BF16),
        in_specs=[smem] + [vmem] * 13 + [smem],
        out_specs=vmem,
        scratch_shapes=[
            pltpu.VMEM((n_i + n_j, 64, res), BF16),
            pltpu.VMEM((n_i, 128, res), BF16),
            pltpu.VMEM((n_i, 128, res), BF16),
        ],
        compiler_params=pltpu.CompilerParams(vmem_limit_bytes=48 * 2**20),
        name="pair_block",
    )(
        starts, left3, rrhs, wp3, base, wd1, rel, tri_gain[:, None],
        sides[0], sides[1], w_gate, jnp.concatenate([w_tri_out, w_tri_out], axis=0),
        out_gain[:, None, None], mask.astype(F32)[None], mask,
    )
    rows = n_i // 2
    theirs = lax.dynamic_slice_in_dim(block, (1 - core) * rows, rows, 0)
    own = lax.dynamic_slice_in_dim(block, core * rows, rows, 0)
    other = partner(theirs, "core", NC, 1)
    return jnp.where(
        core == 0, jnp.concatenate([own, other], axis=1), jnp.concatenate([other, own], axis=1)
    )


def pair_vectors(states, token_start, lnf_gain, w_pair, pair_start):
    count = states.shape[0]
    mp = lax.axis_index("mp")
    weight = lnf_gain[:, None] * w_pair.astype(F32)
    high, low = split(weight)
    table = jnp.concatenate([high, low, jnp.ones((weight.shape[0], 8), BF16)], axis=1)
    dots = lax.dot_general(table, states, (((0,), (1,)), ((), ())), preferred_element_type=F32)
    states32 = states.astype(F32)
    second = jnp.sum(states32 * states32, axis=1)
    lanes = count // NY
    shift_row = jnp.pad(jnp.sum(weight, axis=0), (0, lanes - 64))
    rows = jnp.concatenate([dots[:64] + dots[64:128], dots[128:129], second[None]], axis=0)
    parts = jnp.concatenate(
        [
            jnp.swapaxes(rows.reshape(66, NY, lanes), 0, 1),
            jnp.broadcast_to(shift_row, (NY, 1, lanes)),
            jnp.zeros((NY, 5, lanes), F32),
        ],
        axis=1,
    )
    total = lax.dynamic_index_in_dim(parts, mp, 0, False)
    for by in range(1, NY):
        total = total + shift(
            lax.dynamic_index_in_dim(parts, (mp + by) % NY, 0, False), "mp", NY, by
        )
    full_width = weight.shape[0] * NY
    center = total[64] / full_width
    spread = total[65] / full_width - center * center
    vectors = (total[:64] - total[66, :64][:, None] * center[None]) * lax.rsqrt(spread + EPS)[None]
    place = token_start + mp * lanes + jnp.arange(lanes, dtype=jnp.int32)
    wanted = (place >= pair_start) & (place < pair_start + count)
    vectors = jnp.where(wanted[None], vectors, 0.0)
    vectors = vectors + partner(vectors, "core", NC, 1)
    vectors = sum([shift(vectors, "x", NX, by) for by in range(1, NX)], vectors)
    for bit in (1, 2, 4):
        vectors = vectors + partner(vectors, "z", NZ, bit)
    around = [vectors] + [shift(vectors, "mp", NY, -by) for by in range(1, NY)]
    ring = jnp.concatenate(around + around, axis=1)
    return lax.dynamic_slice_in_dim(ring, (pair_start - mp * lanes) % count, count, 1)


def shards(
    tokens,
    ln1_gain,
    w_query,
    w_key,
    w_value,
    w_out,
    segment_ids,
    lnf_gain,
    w_pair,
    pair_start,
    residue_mask,
    w_pair_out,
    rel_table,
    tri_gain,
    w_ap,
    w_ag,
    w_bp,
    w_bg,
    w_gate,
    out_gain,
    w_tri_out,
):
    mp_index = lax.axis_index("mp")
    seq_index = (lax.axis_index("z") * NX + lax.axis_index("x")) * NC + lax.axis_index("core")
    count = tokens.shape[0]

    groups = ((0, 3), (3, 5))
    weights = lax.all_gather(by_group(w_query, w_key, w_value, groups), SEQ, axis=0, tiled=True)
    normed_tokens = norm_rows(tokens.astype(F32), ln1_gain).astype(BF16)
    sides = jnp.stack([w_ag.T, w_ap.T, w_bg.T, w_bp.T])
    sides = in_order([sides] + [shift(sides, "mp", NY, -by) for by in range(1, NY)], mp_index, 1)
    normed_tokens, sides = lax.optimization_barrier((normed_tokens, sides))
    sides = (sides[:2].reshape(128, 128), sides[2:].reshape(128, 128))
    cosine, sine = angles_of(segment_ids, HD)

    own = w_query.shape[1]
    local_width = w_out.shape[1]
    total = lax.dynamic_slice_in_dim(tokens, mp_index * local_width, local_width, 1).astype(F32)

    def exchange(mixed):
        half = count // 2
        up, down = shift(mixed, "mp", NY, 1), shift(mixed, "mp", NY, -1)
        far = jnp.concatenate(
            [shift(up[:half], "mp", NY, 1), shift(down[half:], "mp", NY, -1)], axis=0
        )
        return [(mixed, 0), (up, -1), (down, 1), (far, 2)]

    def output_part(total, mixed, start):
        for held, by in exchange(mixed):
            row = (mp_index + by) % NY * own + start
            rows = lax.dynamic_slice_in_dim(w_out, row, held.shape[1], 0)
            total = total + jnp.dot(held, rows, preferred_element_type=F32)
        return total

    def own_heads(rows, first, last):
        count = last - first
        cut = slice(first * 3 * HD, last * 3 * HD)
        projected = jnp.dot(rows, weights[:, cut], preferred_element_type=F32)
        heads = []
        for index in range(count):
            one = [
                projected[:, (part * count + index) * HD : (part * count + index + 1) * HD][None]
                for part in range(3)
            ]
            heads.append(attend(*one, cosine, sine, segment_ids)[0])
        return jnp.concatenate(heads, axis=1)

    mixed = own_heads(normed_tokens, *groups[0])
    total = output_part(total, mixed, 0)
    rows, mixed = lax.optimization_barrier((normed_tokens, mixed))
    total = output_part(total, own_heads(rows, *groups[1]), groups[1][0] * HD)
    final_states = total.astype(BF16)
    pair_t = pair_vectors(final_states, seq_index * count, lnf_gain, w_pair, pair_start[0])
    pair_update = pair_phase(
        pair_t, w_pair_out, rel_table, tri_gain, sides, w_gate, w_tri_out, out_gain, residue_mask
    )
    return (final_states, pair_update)


def solution(mesh):
    split_mesh = Mesh(mesh.devices.reshape(NZ, NX, NC, NY), ("z", "x", "core", "mp"))
    return jax.shard_map(
        shards,
        mesh=split_mesh,
        in_specs=(
            P(SEQ, None),
            P(),
            P(SEQ, "mp"),
            P(SEQ, "mp"),
            P(SEQ, "mp"),
            P(None, "mp"),
            P(SEQ, None),
            P("mp"),
            P("mp", None),
            P(),
            P(),
            P(),
            P(),
            P(),
            P(None, "mp"),
            P(None, "mp"),
            P(None, "mp"),
            P(None, "mp"),
            P(),
            P(),
            P(),
        ),
        out_specs=(P(SEQ, "mp"), P(SEQ, "mp", None)),
        check_vma=False,
    )
```
